32 devices in a mesh: dap: 4 (over x, core), slab: 8 (over z, y).
Axes of the slice: x: 2, y: 2, z: 4, core: 2. Of those that a mesh axis runs over, the one named last changes fastest.
Arguments:
- pair: bfloat16 [32, 32, 128], P('dap', 'slab'), may hold values from -6 to 6
- chain_lengths: int32 [8], replicated, may hold values from 1 to 4, as said below
- norm_gains: float32 [3, 128], replicated, may hold values from 0.25 to 1.75
- w_tri_in: bfloat16 [128, 640], replicated, may hold values from -0.5 to 0.5
- w_tri_out: bfloat16 [128, 128], replicated, may hold values from -0.5 to 0.5
- w_bias: bfloat16 [128, 4], replicated, may hold values from -0.5 to 0.5
- w_att_in: bfloat16 [128, 512], replicated
- w_att_out: bfloat16 [128, 128], replicated, may hold values from -0.5 to 0.5
Outputs:
- result: bfloat16 [32, 32, 128], P(None, ('slab', 'dap'))
The draws below stay inside these ranges and needn't reach their ends.
Inputs may be any that keep to these rules, and one draw needn't show every extreme that they name: `chain_lengths`: chain c owns token slots c * 4 to (c + 1) * 4 - 1; slots past its length are padding.
All inputs are finite; a program needn't handle non-finite values.
Results may differ from the reference program's by a relative error of at most 0.012.
Values may be sent and summed in bfloat16 or wider, within the bound.
A program may use at most 64 MiB of HBM per device.

```python
import math
import jax
import jax.numpy as jnp
from jax import lax

C = 128
H = 4
DH = 32
CHAINS = 8
TOKENS = 32
ROW_BLOCK = 8
SLOT = 4


def draw_chain_lengths(key, part):
    draw_keys = jax.random.split(jax.random.fold_in(key, 3), 2)
    lengths = jax.random.randint(draw_keys[0], (CHAINS,), SLOT // 4, SLOT + 1, dtype=jnp.int32)
    chain_order = jax.random.permutation(draw_keys[1], CHAINS)
    chain_slots = jnp.arange(CHAINS, dtype=jnp.int32)
    lengths = jnp.where(chain_slots == chain_order[0], SLOT, lengths)
    lengths = jnp.where(chain_slots == chain_order[1], SLOT // 4, lengths)
    return lengths.astype(jnp.int32)


def draw_w_att_in(key, part):
    att_width = H * DH
    draw_keys = jax.random.split(jax.random.fold_in(key, 7), 1)
    drawn_draw = jax.random.normal(draw_keys[0], (C, 4 * att_width), jnp.float32) / math.sqrt(C)
    return drawn_draw.astype(jnp.bfloat16)


def block_scale(key, extent, cuts, low, high):
    def one(dim, blocks):
        steps = jax.random.uniform(jax.random.fold_in(jax.random.fold_in(key, 6), dim), (blocks,), jnp.float32, low / len(cuts), high / len(cuts))
        return jnp.repeat(jnp.exp(steps), extent[dim] // blocks).reshape((-1,) + (1,) * (len(extent) - dim - 1))

    gain = one(*cuts[0])
    for cut in cuts[1:]:
        gain = gain * one(*cut)
    return gain


def gaussian(rng, dims, width, reach, pieces=(), kind=jnp.bfloat16):
    array = width * jax.random.normal(rng, dims, jnp.float32)
    if pieces:
        array = array * block_scale(rng, dims, pieces, -0.22, 0.18)
    return jnp.clip(array, -reach, reach).astype(kind)


def setup_inputs(seed: int = 0) -> dict:
    keys = jax.random.split(jax.random.key(seed), 9)
    pair = gaussian(keys[0], (TOKENS, TOKENS, C), 1.0, 6.0, ((0, 4), (1, 8)))
    chain_lengths = draw_chain_lengths(jax.random.fold_in(keys[8], 71), 0)
    norm_gains = jnp.clip(1.0 + 0.15 * jax.random.normal(keys[2], (3, C), jnp.float32), 0.25, 1.75)
    w_tri_in = gaussian(keys[3], (C, 5 * C), C ** -0.5, 0.5)
    w_tri_out = gaussian(keys[4], (C, C), C ** -0.5, 0.5)
    w_bias = gaussian(keys[5], (C, H), C ** -0.5, 0.5)
    w_att_in = draw_w_att_in(jax.random.fold_in(keys[8], 71), 0)
    w_att_out = gaussian(keys[7], (H * DH, C), (H * DH) ** -0.5, 0.5)
    return {"pair": pair, "chain_lengths": chain_lengths, "norm_gains": norm_gains, "w_tri_in": w_tri_in, "w_tri_out": w_tri_out, "w_bias": w_bias, "w_att_in": w_att_in, "w_att_out": w_att_out}


EPSILON = 1e-05

def layer_norm(values, gain_row):
    average = lax.optimization_barrier(jnp.mean(values, axis=-1, keepdims=True))
    centred = values - average
    spread = lax.optimization_barrier(jnp.mean(centred * centred, axis=-1, keepdims=True))
    return centred * lax.rsqrt(spread + EPSILON) * gain_row

def token_valid(chain_lengths, first_token, token_count, slot_size):
    token_index = first_token + jnp.arange(token_count, dtype=jnp.int32)
    chain_index = token_index // slot_size
    member = chain_index[:, None] == jnp.arange(chain_lengths.shape[0], dtype=jnp.int32)[None, :]
    chain_limit = lax.optimization_barrier(jnp.sum(jnp.where(member, chain_lengths[None, :], 0), axis=1))
    return (token_index % slot_size < chain_limit).astype(jnp.float32)

def project(values, weight):
    flattened = values.reshape(-1, values.shape[-1])
    product = jnp.dot(flattened, weight, preferred_element_type=jnp.float32)
    return product.reshape(values.shape[:-1] + (weight.shape[1],))

def reference(pair, chain_lengths, norm_gains, w_tri_in, w_tri_out, w_bias, w_att_in, w_att_out):
    token_mask = token_valid(chain_lengths, 0, TOKENS, SLOT)
    blocks = TOKENS // ROW_BLOCK
    pair_blocks = pair.reshape(blocks, ROW_BLOCK, TOKENS, C)
    mask_blocks = token_mask.reshape(blocks, ROW_BLOCK)

    def edge_panels(packed):
        row_block, row_valid = packed
        normed = layer_norm(row_block.astype(jnp.float32), norm_gains[0]).astype(jnp.bfloat16)
        projected = project(normed, w_tri_in)
        pair_mask = (row_valid[:, None] * token_mask[None, :])[:, :, None]
        left_edges = (pair_mask * jax.nn.sigmoid(projected[..., C:2 * C]) * projected[..., :C]).astype(jnp.bfloat16)
        right_edges = (pair_mask * jax.nn.sigmoid(projected[..., 3 * C:4 * C]) * projected[..., 2 * C:3 * C]).astype(jnp.bfloat16)
        return (left_edges, right_edges)
    left_edges, right_edges = lax.map(edge_panels, (pair_blocks, mask_blocks))
    right_all = right_edges.reshape(TOKENS, TOKENS, C).astype(jnp.float32)

    def update_rows(packed):
        row_block, left_rows = packed
        triangle = jnp.einsum('ikc,jkc->ijc', left_rows.astype(jnp.float32), right_all, precision=lax.Precision.HIGHEST)
        normed = layer_norm(row_block.astype(jnp.float32), norm_gains[0]).astype(jnp.bfloat16)
        out_gate = jax.nn.sigmoid(project(normed, w_tri_in[:, 4 * C:]))
        normed_tri = layer_norm(triangle, norm_gains[1]).astype(jnp.bfloat16)
        mixed_update = out_gate * project(normed_tri, w_tri_out)
        return (row_block.astype(jnp.float32) + mixed_update).astype(jnp.bfloat16)
    updated = lax.map(update_rows, (pair_blocks, left_edges)).reshape(TOKENS, TOKENS, C)
    att_width = H * DH
    score_scale = 1.0 / math.sqrt(DH)

    def attention_inputs(row_block):
        normed = layer_norm(row_block.astype(jnp.float32), norm_gains[2]).astype(jnp.bfloat16)
        projected = project(normed, w_att_in)
        pair_bias = project(normed, w_bias).astype(jnp.bfloat16)
        return (projected[..., :3 * att_width].astype(jnp.bfloat16), jax.nn.sigmoid(projected[..., 3 * att_width:]), pair_bias)
    streams, att_gate, pair_bias = lax.map(attention_inputs, updated.reshape(blocks, ROW_BLOCK, TOKENS, C))
    streams = streams.reshape(TOKENS, TOKENS, 3 * att_width)
    att_gate = att_gate.reshape(TOKENS, TOKENS, att_width)
    bias_heads = jnp.transpose(pair_bias.reshape(TOKENS, TOKENS, H), (2, 0, 1)).astype(jnp.float32)
    key_valid = (token_mask > 0)[None, :, None]

    def one_column(column):
        stream = lax.dynamic_index_in_dim(streams, column, 1, keepdims=False).astype(jnp.float32)
        query_part = stream[:, :att_width].reshape(TOKENS, H, DH)
        key_part = stream[:, att_width:2 * att_width].reshape(TOKENS, H, DH)
        value_part = stream[:, 2 * att_width:].reshape(TOKENS, H, DH)
        scores = jnp.einsum('khd,ihd->hki', key_part, query_part, precision=lax.Precision.HIGHEST) * score_scale + bias_heads
        scores = jnp.where(key_valid, scores, -1e+30)
        score_top = lax.optimization_barrier(jnp.max(scores, axis=1, keepdims=True))
        weights = jnp.exp(scores - score_top)
        weights = (weights / lax.optimization_barrier(jnp.sum(weights, axis=1, keepdims=True))).astype(jnp.bfloat16)
        attended = jnp.einsum('hki,khd->ihd', weights.astype(jnp.float32), value_part, precision=lax.Precision.HIGHEST).reshape(TOKENS, att_width)
        gate_column = lax.dynamic_index_in_dim(att_gate, column, 1, keepdims=False)
        gated = (gate_column * attended).astype(jnp.bfloat16)
        residual = lax.dynamic_index_in_dim(updated, column, 1, keepdims=False).astype(jnp.float32)
        return (residual + jnp.dot(gated, w_att_out, preferred_element_type=jnp.float32)).astype(jnp.bfloat16)
    result = lax.map(one_column, jnp.arange(TOKENS, dtype=jnp.int32))
    return jnp.transpose(result, (1, 0, 2))
```

```python
import functools
import math

import jax
import jax.numpy as jnp
from jax import lax
from jax.experimental import pallas as pl
from jax.experimental.pallas import tpu as pltpu
from jax.sharding import PartitionSpec as P

MESH = pl.DeviceIdType.MESH
F32 = jnp.float32
BF16 = jnp.bfloat16

EPSILON = 1e-05


def spread_2(value, axis, source):
    kept = jnp.where(lax.axis_index(axis) == source, value, 0).astype(value.dtype)
    return lax.psum(kept, axis)


def layer_norm(values, gain_row):
    average = jnp.mean(values, axis=-1, keepdims=True)
    centred = values - average
    spread = jnp.mean(centred * centred, axis=-1, keepdims=True)
    return centred * lax.rsqrt(spread + EPSILON) * gain_row


def token_valid(chain_lengths, first_token, token_count, slot_size):
    token_index = first_token + jnp.arange(token_count, dtype=jnp.int32)
    chain_index = token_index // slot_size
    member = chain_index[:, None] == jnp.arange(chain_lengths.shape[0], dtype=jnp.int32)[None, :]
    chain_limit = jnp.sum(jnp.where(member, chain_lengths[None, :], 0), axis=1)
    return (token_index % slot_size < chain_limit).astype(jnp.float32)


def on_device(pair, chain_lengths, norm_gains, w_tri_in, w_tri_out, w_bias, w_att_in, w_att_out):
    row_count, col_count, channels = pair.shape
    dap_size = lax.axis_size("dap")
    slab_size = lax.axis_size("slab")
    tokens = row_count * dap_size
    slot_size = tokens // chain_lengths.shape[0]
    dap_index = lax.axis_index("dap")
    slab_index = lax.axis_index("slab")
    row_valid = token_valid(chain_lengths, dap_index * row_count, row_count, slot_size)
    col_valid = token_valid(chain_lengths, slab_index * col_count, col_count, slot_size)
    normed = layer_norm(pair.astype(jnp.float32), norm_gains[0]).astype(jnp.bfloat16)
    projected = jnp.dot(normed, w_tri_in, preferred_element_type=jnp.float32)
    out_gate = jax.nn.sigmoid(projected[..., 4 * channels :])
    normed_all = lax.all_gather(normed, "slab", axis=1, tiled=True)
    slab_ratio = slab_size // dap_size
    offset = slab_index % slab_ratio * col_count
    own_normed = lax.dynamic_slice_in_dim(normed_all, offset, col_count, 0)
    right_normed = spread_2(own_normed, "dap", slab_index // slab_ratio)
    all_valid = token_valid(chain_lengths, 0, tokens, slot_size)
    span = min(128, tokens)
    w_left = w_tri_in[:, : 2 * channels]
    w_right = w_tri_in[:, 2 * channels : 4 * channels]

    def add_span(step, running):
        first = step * span
        k_valid = lax.dynamic_slice_in_dim(all_valid, first, span, 0)
        left_in = lax.dynamic_slice_in_dim(normed_all, first, span, 1)
        right_in = lax.dynamic_slice_in_dim(right_normed, first, span, 1)
        left_proj = jnp.dot(left_in, w_left, preferred_element_type=jnp.float32)
        right_proj = jnp.dot(right_in, w_right, preferred_element_type=jnp.float32)
        left_mask = (row_valid[:, None] * k_valid[None, :])[:, :, None]
        right_mask = (col_valid[:, None] * k_valid[None, :])[:, :, None]
        left_block = (
            left_mask * jax.nn.sigmoid(left_proj[..., channels:]) * left_proj[..., :channels]
        ).astype(jnp.bfloat16)
        right_block = (
            right_mask * jax.nn.sigmoid(right_proj[..., channels:]) * right_proj[..., :channels]
        ).astype(jnp.bfloat16)
        return running + jnp.einsum(
            "ikc,jkc->ijc", left_block, right_block, preferred_element_type=jnp.float32
        )

    triangle = lax.fori_loop(
        0, tokens // span, add_span, jnp.zeros((row_count, col_count, channels), jnp.float32)
    )
    normed_tri = layer_norm(triangle, norm_gains[1]).astype(jnp.bfloat16)
    mixed_update = out_gate * jnp.dot(normed_tri, w_tri_out, preferred_element_type=jnp.float32)
    updated = (pair.astype(jnp.float32) + mixed_update).astype(jnp.bfloat16)
    columns = lax.all_to_all(updated, "dap", split_axis=1, concat_axis=0, tiled=True)
    normed_cols = layer_norm(columns.astype(jnp.float32), norm_gains[2]).astype(jnp.bfloat16)
    normed_rows = layer_norm(updated.astype(jnp.float32), norm_gains[2]).astype(jnp.bfloat16)
    bias_block = jnp.einsum(
        "ijc,ch->hij", normed_rows, w_bias, preferred_element_type=jnp.float32
    ).astype(jnp.bfloat16)
    bias_tall = lax.all_gather(bias_block, "dap", axis=1, tiled=True)
    pair_bias = lax.all_gather(bias_tall, "slab", axis=2, tiled=True)
    att_projected = jnp.dot(normed_cols, w_att_in, preferred_element_type=jnp.float32)
    att_width = w_att_out.shape[0]
    head_count = w_bias.shape[1]
    head_dim = att_width // head_count
    score_scale = 1.0 / math.sqrt(head_dim)
    query_rows = att_projected[..., :att_width].astype(jnp.bfloat16)
    key_rows = att_projected[..., att_width : 2 * att_width].astype(jnp.bfloat16)
    value_rows = att_projected[..., 2 * att_width : 3 * att_width].astype(jnp.bfloat16)
    att_gate = jax.nn.sigmoid(att_projected[..., 3 * att_width :])
    key_valid = token_valid(chain_lengths, 0, tokens, slot_size)[:, None] > 0
    head_outputs = []
    for head_index in range(head_count):
        head_start = head_index * head_dim
        query_head = query_rows[:, 0, head_start : head_start + head_dim]
        key_head = key_rows[:, 0, head_start : head_start + head_dim]
        value_head = value_rows[:, 0, head_start : head_start + head_dim]
        scores = lax.dot_general(
            key_head, query_head, (((1,), (1,)), ((), ())), preferred_element_type=jnp.float32
        ) * score_scale + pair_bias[head_index].astype(jnp.float32)
        scores = jnp.where(key_valid, scores, -1e30)
        score_top = jnp.max(scores, axis=0, keepdims=True)
        weights = jnp.exp(scores - score_top)
        weights = (weights / jnp.sum(weights, axis=0, keepdims=True)).astype(jnp.bfloat16)
        head_outputs.append(
            lax.dot_general(
                weights, value_head, (((0,), (0,)), ((), ())), preferred_element_type=jnp.float32
            )
        )
    column_results = [jnp.concatenate(head_outputs, axis=1)]
    attended = jnp.stack(column_results, axis=1)
    gated = (att_gate * attended).astype(jnp.bfloat16)
    return (
        columns.astype(jnp.float32) + jnp.dot(gated, w_att_out, preferred_element_type=jnp.float32)
    ).astype(jnp.bfloat16)


def small_kernel(
    dap_size, slab_size, slot_size,
    pair_hbm, len_hbm, gains_hbm, w_in_hbm, w_out_hbm, w_bias_hbm, w_att_hbm, w_ao_hbm,
    out_ref,
    pair_v, len_s, gains_v, w_in_v, w_out_v, w_bias_v, w_att_v, w_ao_v,
    x_scr, left_buf, right_own, right_buf, right_f32, upd_own, col_buf, bias_buf,
    in_sem, left_send, left_recv, right_send, right_recv,
    col_send, col_recv, bias_send, bias_recv,
):
    rows, cols, channels = pair_hbm.shape
    block = rows * cols
    tokens = rows * dap_size
    devices = dap_size * slab_size
    ratio = rows // cols
    a = lax.axis_index("dap")
    s = lax.axis_index("slab")
    me = s * dap_size + a

    def place(index):
        return (lax.rem(index, dap_size), lax.div(index, dap_size))

    barrier = pltpu.get_barrier_semaphore()

    def greet(d, carry):
        pl.semaphore_signal(
            barrier, inc=1, device_id=place(lax.rem(me + d, devices)), device_id_type=MESH
        )
        return carry

    pairs = (
        (pair_hbm, pair_v), (len_hbm, len_s), (gains_hbm, gains_v), (w_in_hbm, w_in_v),
        (w_bias_hbm, w_bias_v), (w_out_hbm, w_out_v), (w_att_hbm, w_att_v), (w_ao_hbm, w_ao_v),
    )
    loads = [pltpu.make_async_copy(src, dst, in_sem.at[n]) for n, (src, dst) in enumerate(pairs)]
    for load in loads:
        load.start()
    lax.fori_loop(1, devices, greet, 0, unroll=True)

    for load in loads[:4]:
        load.wait()

    row = lax.broadcasted_iota(jnp.int32, (block, channels), 0)
    lane = lax.broadcasted_iota(jnp.int32, (block, channels), 1)
    row_shift = rows.bit_length() - 1
    col_shift = cols.bit_length() - 1

    def valid(token):
        inside = None
        for chain in range(len_hbm.shape[0]):
            first = chain * slot_size
            here = jnp.logical_and(token >= first, token < first + len_s[chain])
            inside = here if inside is None else jnp.logical_or(inside, here)
        return inside

    def norm(values, gain):
        return layer_norm(values, gains_v[gain : gain + 1, :])

    def dot(x, y):
        return jnp.dot(x, y, preferred_element_type=F32)

    for i in range(rows):
        x_scr[i * cols : (i + 1) * cols, :] = pair_v[i].astype(F32)
    x_nat = x_scr[...]
    x_perm = jnp.concatenate([x_scr[pl.ds(k, rows, stride=cols), :] for k in range(cols)], axis=0)
    normed_nat = norm(x_nat, 0).astype(BF16)
    normed_perm = norm(x_perm, 0).astype(BF16)
    mask_nat = jnp.logical_and(
        valid(a * rows + lax.shift_right_logical(row, col_shift)),
        valid(s * cols + (row & (cols - 1))),
    ).astype(F32)
    mask_perm = jnp.logical_and(
        valid(a * rows + (row & (rows - 1))),
        valid(s * cols + lax.shift_right_logical(row, row_shift)),
    ).astype(F32)
    left_proj = dot(normed_perm, w_in_v[:, : 2 * channels])
    right_proj = dot(normed_nat, w_in_v[:, 2 * channels : 4 * channels])
    left_buf[s] = (
        mask_perm * jax.nn.sigmoid(left_proj[:, channels:]) * left_proj[:, :channels]
    ).astype(BF16)
    right_own[...] = (
        (mask_nat * jax.nn.sigmoid(right_proj[:, channels:]) * right_proj[:, :channels])
        .astype(BF16)
        .reshape(ratio, block // ratio, channels)
    )

    pl.semaphore_wait(barrier, devices - 1)

    def send_left(d, carry):
        pltpu.make_async_remote_copy(
            src_ref=left_buf.at[s],
            dst_ref=left_buf.at[s],
            send_sem=left_send,
            recv_sem=left_recv,
            device_id=(a, lax.rem(s + d, slab_size)),
            device_id_type=MESH,
        ).start()
        return carry

    def right_copies():
        for part in range(ratio):
            for d in range(dap_size):
                to_a = lax.rem(a + d, dap_size)
                to_s = a * ratio + part
                remote = pltpu.make_async_remote_copy(
                    src_ref=right_own.at[part],
                    dst_ref=right_buf.at[s],
                    send_sem=right_send.at[part * dap_size + d],
                    recv_sem=right_recv,
                    device_id=(to_a, to_s),
                    device_id_type=MESH,
                )
                local = None
                if d == 0:
                    local = pltpu.make_async_copy(right_own.at[part], right_buf.at[s], right_recv)
                yield to_s, remote, local

    lax.fori_loop(1, slab_size, send_left, 0, unroll=True)
    for to_s, remote, local in right_copies():
        if local is None:
            remote.start()
        else:
            pl.when(to_s == s)(local.start)
            pl.when(to_s != s)(remote.start)

    out_gate = jax.nn.sigmoid(dot(normed_perm, w_in_v[:, 4 * channels :]))
    loads[4].wait()
    heads = w_bias_hbm.shape[1]
    head_dim = channels // heads
    head_shift = head_dim.bit_length() - 1
    spread_row = lax.broadcasted_iota(jnp.int32, (heads, channels), 0)
    spread_lane = lax.broadcasted_iota(jnp.int32, (heads, channels), 1)
    spread = (lax.shift_right_logical(spread_lane, head_shift) == spread_row).astype(F32)
    w_bias_wide = dot(w_bias_v[...], spread.astype(BF16)).astype(BF16)
    key_ok = valid(lane & (tokens - 1))
    lane_head = lax.shift_right_logical(lane, head_shift)
    for load in loads[5:]:
        load.wait()

    pltpu.make_async_copy(right_buf, right_buf, right_recv).wait()
    right_f32[...] = right_buf[...].astype(F32).reshape(right_f32.shape)
    others = left_buf.at[pl.ds(0, slab_size - 1)]
    pltpu.make_async_copy(others, others, left_recv).wait()
    triangle = [jnp.zeros((rows, channels), F32) for _ in range(cols)]
    for k_block in range(slab_size):
        left = left_buf[k_block].astype(F32)
        for k in range(cols):
            left_k = left[k * rows : (k + 1) * rows, :]
            for j in range(cols):
                at = k_block * cols * cols + j * cols + k
                triangle[j] += left_k * right_f32[at : at + 1, :]
    triangle = jnp.concatenate(triangle, axis=0)
    normed_tri = norm(triangle, 1).astype(BF16)
    updated = (x_perm + out_gate * dot(normed_tri, w_out_v[...])).astype(BF16).astype(F32)
    upd_own[...] = updated.reshape(upd_own.shape)
    col_buf[a] = upd_own[a]

    def col_copy(d):
        to_a = lax.rem(a + d, dap_size)
        return pltpu.make_async_remote_copy(
            src_ref=upd_own.at[to_a],
            dst_ref=col_buf.at[a],
            send_sem=col_send.at[d - 1],
            recv_sem=col_recv,
            device_id=(to_a, s),
            device_id_type=MESH,
        )

    for d in range(1, dap_size):
        col_copy(d).start()

    normed_local = norm(updated, 2).astype(BF16)
    bias_all = dot(normed_local, w_bias_wide)
    bias_row = jnp.sum(
        jnp.where((lane & (block - 1)) == row, bias_all, 0.0), axis=0, keepdims=True
    )
    bias_buf[me] = bias_row.astype(BF16).astype(F32)

    def send_bias(d, carry):
        pltpu.make_async_remote_copy(
            src_ref=bias_buf.at[me],
            dst_ref=bias_buf.at[me],
            send_sem=bias_send,
            recv_sem=bias_recv,
            device_id=place(lax.rem(me + d, devices)),
            device_id_type=MESH,
        ).start()
        return carry

    lax.fori_loop(1, devices, send_bias, 0, unroll=True)

    other_cols = col_buf.at[pl.ds(0, dap_size - 1)]
    pltpu.make_async_copy(other_cols, other_cols, col_recv).wait()
    columns = col_buf[...].reshape(tokens, channels)
    normed_cols = norm(columns, 2).astype(BF16)
    projected = dot(normed_cols, w_att_v[...])
    query = projected[:, :channels].astype(BF16)
    key = projected[:, channels : 2 * channels].astype(BF16)
    value = projected[:, 2 * channels : 3 * channels].astype(BF16)
    att_gate = jax.nn.sigmoid(projected[:, 3 * channels :])
    blank = jnp.zeros_like(key)
    key_wide = jnp.concatenate([jnp.where(lane_head == h, key, blank) for h in range(heads)], axis=0)
    value_wide = jnp.concatenate(
        [jnp.where(lane_head == h, value, blank) for h in range(heads)], axis=0
    )
    scores = lax.dot_general(
        query, key_wide, (((1,), (1,)), ((), ())), preferred_element_type=F32
    ) * (1.0 / math.sqrt(head_dim))

    other_rows = bias_buf.at[pl.ds(0, devices - 1)]
    pltpu.make_async_copy(other_rows, other_rows, bias_recv).wait()
    got = bias_buf[:, 0, :]
    shift = (row & (cols - 1)) - (lax.shift_right_logical(lane, row_shift) & (dap_size - 1))
    bias = got
    for delta in range(1 - cols, cols):
        if delta:
            moved = pltpu.roll(got, delta % tokens, 0)
            moved = pltpu.roll(moved, (-rows * delta) % channels, 1)
            bias = jnp.where(shift == delta, moved, bias)
    scores = jnp.where(key_ok, scores + bias, -1e30)
    top = jnp.zeros_like(scores)
    for h in range(heads):
        here = lane_head == h
        top = jnp.where(
            here, jnp.max(jnp.where(here, scores, -jnp.inf), axis=1, keepdims=True), top
        )
    weights = jnp.exp(scores - top)
    total = jnp.zeros_like(scores)
    for h in range(heads):
        here = lane_head == h
        total = jnp.where(here, jnp.sum(jnp.where(here, weights, 0.0), axis=1, keepdims=True), total)
    weights = (weights / total).astype(BF16)
    gated = (att_gate * dot(weights, value_wide)).astype(BF16)
    out_ref[...] = columns + dot(gated, w_ao_v[...])

    pltpu.make_async_copy(others, others, left_send).wait()
    for to_s, remote, local in right_copies():
        if local is None:
            remote.wait_send()
        else:
            pl.when(to_s != s)(remote.wait_send)
    for d in range(1, dap_size):
        col_copy(d).wait_send()
    pltpu.make_async_copy(other_rows, other_rows, bias_send).wait()


def on_device_small(*args):
    pair, chain_lengths = args[:2]
    rows, cols, channels = pair.shape
    dap_size = lax.axis_size("dap")
    slab_size = lax.axis_size("slab")
    tokens = rows * dap_size
    devices = dap_size * slab_size
    block = rows * cols
    ratio = rows // cols
    spaces = [pltpu.VMEM] * 8
    spaces[1] = pltpu.SMEM
    result = pl.pallas_call(
        functools.partial(small_kernel, dap_size, slab_size, tokens // chain_lengths.shape[0]),
        out_shape=jax.ShapeDtypeStruct((tokens, channels), F32),
        in_specs=[pl.BlockSpec(memory_space=pl.ANY)] * 8,
        out_specs=pl.BlockSpec(memory_space=pltpu.VMEM),
        scratch_shapes=[space(arg.shape, arg.dtype) for space, arg in zip(spaces, args)]
        + [
            pltpu.VMEM((block, channels), F32),
            pltpu.VMEM((slab_size, block, channels), BF16),
            pltpu.VMEM((ratio, block // ratio, channels), BF16),
            pltpu.VMEM((slab_size, block // ratio, channels), BF16),
            pltpu.VMEM((slab_size * block // ratio, channels), F32),
            pltpu.VMEM((cols, rows, channels), F32),
            pltpu.VMEM((dap_size, rows, channels), F32),
            pltpu.VMEM((devices, 1, channels), F32),
            pltpu.SemaphoreType.DMA((8,)),
            pltpu.SemaphoreType.DMA,
            pltpu.SemaphoreType.DMA,
            pltpu.SemaphoreType.DMA((ratio * dap_size,)),
            pltpu.SemaphoreType.DMA,
            pltpu.SemaphoreType.DMA((dap_size - 1,)),
            pltpu.SemaphoreType.DMA,
            pltpu.SemaphoreType.DMA,
            pltpu.SemaphoreType.DMA,
        ],
        compiler_params=pltpu.CompilerParams(collective_id=0, has_side_effects=True),
    )(*args)
    return result.astype(BF16).reshape(tokens, 1, channels)


def fits_small(mesh, shapes):
    pair, lengths, w_bias = shapes[0].shape, shapes[1].shape, shapes[5].shape
    dap_size, slab_size = mesh.shape["dap"], mesh.shape["slab"]
    tokens, width, channels = pair
    rows, cols, heads = tokens // dap_size, width // slab_size, w_bias[1]
    return (
        tokens == width
        and channels == 128
        and rows == 8
        and cols == dap_size == 4
        and tokens == rows * dap_size == cols * slab_size == dap_size * slab_size
        and heads * tokens == channels
        and shapes[7].shape == (channels, channels)
        and tokens % lengths[0] == 0
    )


def solution(mesh):
    in_specs = (P("dap", "slab", None), P(), P(), P(), P(), P(), P(), P())
    out_specs = P(None, ("slab", "dap"), None)

    def run(*args):
        body = on_device_small if fits_small(mesh, args) else on_device
        return jax.shard_map(
            body, mesh=mesh, in_specs=in_specs, out_specs=out_specs, check_vma=False
        )(*args)

    return run
```

```python
import functools
import math

import jax
import jax.numpy as jnp
from jax import lax
from jax.experimental import pallas as pl
from jax.experimental.pallas import tpu as pltpu
from jax.sharding import PartitionSpec as P

MESH = pl.DeviceIdType.MESH
F32 = jnp.float32
BF16 = jnp.bfloat16

EPSILON = 1e-05


def spread_2(value, axis, source):
    kept = jnp.where(lax.axis_index(axis) == source, value, 0).astype(value.dtype)
    return lax.psum(kept, axis)


def layer_norm(values, gain_row):
    average = jnp.mean(values, axis=-1, keepdims=True)
    centred = values - average
    spread = jnp.mean(centred * centred, axis=-1, keepdims=True)
    return centred * lax.rsqrt(spread + EPSILON) * gain_row


def token_valid(chain_lengths, first_token, token_count, slot_size):
    token_index = first_token + jnp.arange(token_count, dtype=jnp.int32)
    chain_index = token_index // slot_size
    member = chain_index[:, None] == jnp.arange(chain_lengths.shape[0], dtype=jnp.int32)[None, :]
    chain_limit = jnp.sum(jnp.where(member, chain_lengths[None, :], 0), axis=1)
    return (token_index % slot_size < chain_limit).astype(jnp.float32)


def on_device(pair, chain_lengths, norm_gains, w_tri_in, w_tri_out, w_bias, w_att_in, w_att_out):
    row_count, col_count, channels = pair.shape
    dap_size = lax.axis_size("dap")
    slab_size = lax.axis_size("slab")
    tokens = row_count * dap_size
    slot_size = tokens // chain_lengths.shape[0]
    dap_index = lax.axis_index("dap")
    slab_index = lax.axis_index("slab")
    row_valid = token_valid(chain_lengths, dap_index * row_count, row_count, slot_size)
    col_valid = token_valid(chain_lengths, slab_index * col_count, col_count, slot_size)
    normed = layer_norm(pair.astype(jnp.float32), norm_gains[0]).astype(jnp.bfloat16)
    projected = jnp.dot(normed, w_tri_in, preferred_element_type=jnp.float32)
    out_gate = jax.nn.sigmoid(projected[..., 4 * channels :])
    normed_all = lax.all_gather(normed, "slab", axis=1, tiled=True)
    slab_ratio = slab_size // dap_size
    offset = slab_index % slab_ratio * col_count
    own_normed = lax.dynamic_slice_in_dim(normed_all, offset, col_count, 0)
    right_normed = spread_2(own_normed, "dap", slab_index // slab_ratio)
    all_valid = token_valid(chain_lengths, 0, tokens, slot_size)
    span = min(128, tokens)
    w_left = w_tri_in[:, : 2 * channels]
    w_right = w_tri_in[:, 2 * channels : 4 * channels]

    def add_span(step, running):
        first = step * span
        k_valid = lax.dynamic_slice_in_dim(all_valid, first, span, 0)
        left_in = lax.dynamic_slice_in_dim(normed_all, first, span, 1)
        right_in = lax.dynamic_slice_in_dim(right_normed, first, span, 1)
        left_proj = jnp.dot(left_in, w_left, preferred_element_type=jnp.float32)
        right_proj = jnp.dot(right_in, w_right, preferred_element_type=jnp.float32)
        left_mask = (row_valid[:, None] * k_valid[None, :])[:, :, None]
        right_mask = (col_valid[:, None] * k_valid[None, :])[:, :, None]
        left_block = (
            left_mask * jax.nn.sigmoid(left_proj[..., channels:]) * left_proj[..., :channels]
        ).astype(jnp.bfloat16)
        right_block = (
            right_mask * jax.nn.sigmoid(right_proj[..., channels:]) * right_proj[..., :channels]
        ).astype(jnp.bfloat16)
        return running + jnp.einsum(
            "ikc,jkc->ijc", left_block, right_block, preferred_element_type=jnp.float32
        )

    triangle = lax.fori_loop(
        0, tokens // span, add_span, jnp.zeros((row_count, col_count, channels), jnp.float32)
    )
    normed_tri = layer_norm(triangle, norm_gains[1]).astype(jnp.bfloat16)
    mixed_update = out_gate * jnp.dot(normed_tri, w_tri_out, preferred_element_type=jnp.float32)
    updated = (pair.astype(jnp.float32) + mixed_update).astype(jnp.bfloat16)
    columns = lax.all_to_all(updated, "dap", split_axis=1, concat_axis=0, tiled=True)
    normed_cols = layer_norm(columns.astype(jnp.float32), norm_gains[2]).astype(jnp.bfloat16)
    normed_rows = layer_norm(updated.astype(jnp.float32), norm_gains[2]).astype(jnp.bfloat16)
    bias_block = jnp.einsum(
        "ijc,ch->hij", normed_rows, w_bias, preferred_element_type=jnp.float32
    ).astype(jnp.bfloat16)
    bias_tall = lax.all_gather(bias_block, "dap", axis=1, tiled=True)
    pair_bias = lax.all_gather(bias_tall, "slab", axis=2, tiled=True)
    att_projected = jnp.dot(normed_cols, w_att_in, preferred_element_type=jnp.float32)
    att_width = w_att_out.shape[0]
    head_count = w_bias.shape[1]
    head_dim = att_width // head_count
    score_scale = 1.0 / math.sqrt(head_dim)
    query_rows = att_projected[..., :att_width].astype(jnp.bfloat16)
    key_rows = att_projected[..., att_width : 2 * att_width].astype(jnp.bfloat16)
    value_rows = att_projected[..., 2 * att_width : 3 * att_width].astype(jnp.bfloat16)
    att_gate = jax.nn.sigmoid(att_projected[..., 3 * att_width :])
    key_valid = token_valid(chain_lengths, 0, tokens, slot_size)[:, None] > 0
    head_outputs = []
    for head_index in range(head_count):
        head_start = head_index * head_dim
        query_head = query_rows[:, 0, head_start : head_start + head_dim]
        key_head = key_rows[:, 0, head_start : head_start + head_dim]
        value_head = value_rows[:, 0, head_start : head_start + head_dim]
        scores = lax.dot_general(
            key_head, query_head, (((1,), (1,)), ((), ())), preferred_element_type=jnp.float32
        ) * score_scale + pair_bias[head_index].astype(jnp.float32)
        scores = jnp.where(key_valid, scores, -1e30)
        score_top = jnp.max(scores, axis=0, keepdims=True)
        weights = jnp.exp(scores - score_top)
        weights = (weights / jnp.sum(weights, axis=0, keepdims=True)).astype(jnp.bfloat16)
        head_outputs.append(
            lax.dot_general(
                weights, value_head, (((0,), (0,)), ((), ())), preferred_element_type=jnp.float32
            )
        )
    column_results = [jnp.concatenate(head_outputs, axis=1)]
    attended = jnp.stack(column_results, axis=1)
    gated = (att_gate * attended).astype(jnp.bfloat16)
    return (
        columns.astype(jnp.float32) + jnp.dot(gated, w_att_out, preferred_element_type=jnp.float32)
    ).astype(jnp.bfloat16)


def small_kernel(
    dap_size, slab_size, slot_size,
    pair_hbm, len_hbm, gains_hbm, w_in_hbm, w_out_hbm, w_bias_hbm, w_att_hbm, w_ao_hbm,
    out_ref,
    pair_v, len_s, gains_v, w_in_v, w_out_v, w_bias_v, w_att_v, w_ao_v,
    x_scr, left_buf, right_own, right_buf, right_f32, upd_own, col_buf, bias_buf,
    in_sem, left_send, left_recv, right_send, right_recv,
    col_send, col_recv, bias_send, bias_recv,
):
    rows, cols, channels = pair_hbm.shape
    block = rows * cols
    tokens = rows * dap_size
    devices = dap_size * slab_size
    ratio = rows // cols
    a = lax.axis_index("dap")
    s = lax.axis_index("slab")
    me = s * dap_size + a

    def place(index):
        return (lax.rem(index, dap_size), lax.div(index, dap_size))

    barrier = pltpu.get_barrier_semaphore()

    def greet(d, carry):
        pl.semaphore_signal(
            barrier, inc=1, device_id=place(lax.rem(me + d, devices)), device_id_type=MESH
        )
        return carry

    pairs = (
        (pair_hbm, pair_v), (len_hbm, len_s), (gains_hbm, gains_v), (w_in_hbm, w_in_v),
        (w_bias_hbm, w_bias_v), (w_out_hbm, w_out_v), (w_att_hbm, w_att_v), (w_ao_hbm, w_ao_v),
    )
    loads = [pltpu.make_async_copy(src, dst, in_sem.at[n]) for n, (src, dst) in enumerate(pairs)]
    for load in loads:
        load.start()
    lax.fori_loop(1, devices, greet, 0, unroll=True)

    for load in loads[:4]:
        load.wait()

    row = lax.broadcasted_iota(jnp.int32, (block, channels), 0)
    lane = lax.broadcasted_iota(jnp.int32, (block, channels), 1)
    row_shift = rows.bit_length() - 1
    col_shift = cols.bit_length() - 1

    def valid(token):
        inside = None
        for chain in range(len_hbm.shape[0]):
            first = chain * slot_size
            here = jnp.logical_and(token >= first, token < first + len_s[chain])
            inside = here if inside is None else jnp.logical_or(inside, here)
        return inside

    def norm(values, gain):
        return layer_norm(values, gains_v[gain : gain + 1, :])

    def dot(x, y):
        return jnp.dot(x, y, preferred_element_type=F32)

    for i in range(rows):
        x_scr[i * cols : (i + 1) * cols, :] = pair_v[i].astype(F32)
    x_nat = x_scr[...]
    x_perm = jnp.concatenate([x_scr[pl.ds(k, rows, stride=cols), :] for k in range(cols)], axis=0)
    normed_nat = norm(x_nat, 0).astype(BF16)
    normed_perm = norm(x_perm, 0).astype(BF16)
    mask_nat = jnp.logical_and(
        valid(a * rows + lax.shift_right_logical(row, col_shift)),
        valid(s * cols + (row & (cols - 1))),
    ).astype(F32)
    mask_perm = jnp.logical_and(
        valid(a * rows + (row & (rows - 1))),
        valid(s * cols + lax.shift_right_logical(row, row_shift)),
    ).astype(F32)
    left_proj = dot(normed_perm, w_in_v[:, : 2 * channels])
    right_proj = dot(normed_nat, w_in_v[:, 2 * channels : 4 * channels])
    left_buf[s] = (
        mask_perm * jax.nn.sigmoid(left_proj[:, channels:]) * left_proj[:, :channels]
    ).astype(BF16)
    right_own[...] = (
        (mask_nat * jax.nn.sigmoid(right_proj[:, channels:]) * right_proj[:, :channels])
        .astype(BF16)
        .reshape(ratio, block // ratio, channels)
    )

    pl.semaphore_wait(barrier, devices - 1)

    def send_left(d, carry):
        pltpu.make_async_remote_copy(
            src_ref=left_buf.at[s],
            dst_ref=left_buf.at[s],
            send_sem=left_send,
            recv_sem=left_recv,
            device_id=(a, lax.rem(s + d, slab_size)),
            device_id_type=MESH,
        ).start()
        return carry

    def right_copies():
        for part in range(ratio):
            for d in range(dap_size):
                to_a = lax.rem(a + d, dap_size)
                to_s = a * ratio + part
                remote = lambda part=part, d=d, to_a=to_a, to_s=to_s: pltpu.make_async_remote_copy(
                    src_ref=right_own.at[part],
                    dst_ref=right_buf.at[s],
                    send_sem=right_send.at[part * dap_size + d],
                    recv_sem=right_recv,
                    device_id=(to_a, to_s),
                    device_id_type=MESH,
                )
                yield part, to_s, remote, d == 0

    lax.fori_loop(1, slab_size, send_left, 0, unroll=True)
    for part, to_s, remote, maybe_self in right_copies():
        if not maybe_self:
            remote().start()
        else:
            own = pltpu.make_async_copy(right_own.at[part], right_buf.at[s], right_recv)
            pl.when(to_s == s)(own.start)
            pl.when(to_s != s)(lambda: remote().start())

    out_gate = jax.nn.sigmoid(dot(normed_perm, w_in_v[:, 4 * channels :]))
    loads[4].wait()
    heads = w_bias_hbm.shape[0]
    head_dim = channels // heads
    head_shift = head_dim.bit_length() - 1
    spread_row = lax.broadcasted_iota(jnp.int32, (heads, channels), 0)
    spread_lane = lax.broadcasted_iota(jnp.int32, (heads, channels), 1)
    spread = (lax.shift_right_logical(spread_lane, head_shift) == spread_row).astype(F32)
    w_bias_wide = lax.dot_general(
        w_bias_v[...], spread.astype(BF16), (((0,), (0,)), ((), ())), preferred_element_type=F32
    ).astype(BF16)
    key_ok = valid(lane & (tokens - 1))
    lane_head = lax.shift_right_logical(lane, head_shift)
    for load in loads[5:]:
        load.wait()

    pltpu.make_async_copy(right_buf, right_buf, right_recv).wait()
    right_f32[...] = right_buf[...].astype(F32).reshape(right_f32.shape)
    others = left_buf.at[pl.ds(0, slab_size - 1)]
    pltpu.make_async_copy(others, others, left_recv).wait()
    triangle = [jnp.zeros((rows, channels), F32) for _ in range(cols)]
    for k_block in range(slab_size):
        left = left_buf[k_block].astype(F32)
        for k in range(cols):
            left_k = left[k * rows : (k + 1) * rows, :]
            for j in range(cols):
                at = k_block * cols * cols + j * cols + k
                triangle[j] += left_k * right_f32[at : at + 1, :]
    triangle = jnp.concatenate(triangle, axis=0)
    normed_tri = norm(triangle, 1).astype(BF16)
    updated = (x_perm + out_gate * dot(normed_tri, w_out_v[...])).astype(BF16).astype(F32)
    upd_own[...] = updated.reshape(upd_own.shape)
    col_buf[a] = upd_own[a]

    def col_copy(d):
        to_a = lax.rem(a + d, dap_size)
        return pltpu.make_async_remote_copy(
            src_ref=upd_own.at[to_a],
            dst_ref=col_buf.at[a],
            send_sem=col_send.at[d - 1],
            recv_sem=col_recv,
            device_id=(to_a, s),
            device_id_type=MESH,
        )

    for d in range(1, dap_size):
        col_copy(d).start()

    normed_local = norm(updated, 2).astype(BF16)
    bias_all = dot(normed_local, w_bias_wide)
    bias_row = jnp.sum(
        jnp.where((lane & (block - 1)) == row, bias_all, 0.0), axis=0, keepdims=True
    )
    bias_buf[me] = bias_row.astype(BF16).astype(F32)

    def send_bias(d, carry):
        pltpu.make_async_remote_copy(
            src_ref=bias_buf.at[me],
            dst_ref=bias_buf.at[me],
            send_sem=bias_send,
            recv_sem=bias_recv,
            device_id=place(lax.rem(me + d, devices)),
            device_id_type=MESH,
        ).start()
        return carry

    lax.fori_loop(1, devices, send_bias, 0, unroll=True)

    other_cols = col_buf.at[pl.ds(0, dap_size - 1)]
    pltpu.make_async_copy(other_cols, other_cols, col_recv).wait()
    columns = col_buf[...].reshape(tokens, channels)
    normed_cols = norm(columns, 2).astype(BF16)
    projected = dot(normed_cols, w_att_v[...])
    query = projected[:, :channels].astype(BF16)
    key = projected[:, channels : 2 * channels].astype(BF16)
    value = projected[:, 2 * channels : 3 * channels].astype(BF16)
    att_gate = jax.nn.sigmoid(projected[:, 3 * channels :])
    blank = jnp.zeros_like(key)
    key_wide = jnp.concatenate([jnp.where(lane_head == h, key, blank) for h in range(heads)], axis=0)
    value_wide = jnp.concatenate(
        [jnp.where(lane_head == h, value, blank) for h in range(heads)], axis=0
    )
    scores = lax.dot_general(
        query, key_wide, (((1,), (1,)), ((), ())), preferred_element_type=F32
    ) * (1.0 / math.sqrt(head_dim))

    other_rows = bias_buf.at[pl.ds(0, devices - 1)]
    pltpu.make_async_copy(other_rows, other_rows, bias_recv).wait()
    got = bias_buf[:, 0, :]
    shift = (row & (cols - 1)) - (lax.shift_right_logical(lane, row_shift) & (dap_size - 1))
    bias = got
    for delta in range(1 - cols, cols):
        if delta:
            moved = pltpu.roll(got, delta % tokens, 0)
            moved = pltpu.roll(moved, (-rows * delta) % channels, 1)
            bias = jnp.where(shift == delta, moved, bias)
    scores = jnp.where(key_ok, scores + bias, -1e30)
    top = jnp.zeros_like(scores)
    for h in range(heads):
        here = lane_head == h
        top = jnp.where(
            here, jnp.max(jnp.where(here, scores, -jnp.inf), axis=1, keepdims=True), top
        )
    weights = jnp.exp(scores - top)
    total = jnp.zeros_like(scores)
    for h in range(heads):
        here = lane_head == h
        total = jnp.where(here, jnp.sum(jnp.where(here, weights, 0.0), axis=1, keepdims=True), total)
    weights = (weights / total).astype(BF16)
    gated = (att_gate * dot(weights, value_wide)).astype(BF16)
    out_ref[...] = (columns + dot(gated, w_ao_v[...])).astype(BF16)

    pltpu.make_async_copy(others, others, left_send).wait()
    for part, to_s, remote, maybe_self in right_copies():
        if not maybe_self:
            remote().wait_send()
        else:
            pl.when(to_s != s)(lambda: remote().wait_send())
    for d in range(1, dap_size):
        col_copy(d).wait_send()
    pltpu.make_async_copy(other_rows, other_rows, bias_send).wait()


def on_device_small(*args):
    pair, chain_lengths = args[:2]
    args = args[:5] + (args[5].T,) + args[6:]
    rows, cols, channels = pair.shape
    dap_size = lax.axis_size("dap")
    slab_size = lax.axis_size("slab")
    tokens = rows * dap_size
    devices = dap_size * slab_size
    block = rows * cols
    ratio = rows // cols
    spaces = [pltpu.VMEM] * 8
    spaces[1] = pltpu.SMEM
    result = pl.pallas_call(
        functools.partial(small_kernel, dap_size, slab_size, tokens // chain_lengths.shape[0]),
        out_shape=pltpu.VMEM((tokens, channels), BF16),
        in_specs=[pl.BlockSpec(memory_space=pl.ANY)] * 8,
        out_specs=pl.BlockSpec(memory_space=pltpu.VMEM),
        scratch_shapes=[space(arg.shape, arg.dtype) for space, arg in zip(spaces, args)]
        + [
            pltpu.VMEM((block, channels), F32),
            pltpu.VMEM((slab_size, block, channels), BF16),
            pltpu.VMEM((ratio, block // ratio, channels), BF16),
            pltpu.VMEM((slab_size, block // ratio, channels), BF16),
            pltpu.VMEM((slab_size * block // ratio, channels), F32),
            pltpu.VMEM((cols, rows, channels), F32),
            pltpu.VMEM((dap_size, rows, channels), F32),
            pltpu.VMEM((devices, 1, channels), F32),
            pltpu.SemaphoreType.DMA((8,)),
            pltpu.SemaphoreType.DMA,
            pltpu.SemaphoreType.DMA,
            pltpu.SemaphoreType.DMA((ratio * dap_size,)),
            pltpu.SemaphoreType.DMA,
            pltpu.SemaphoreType.DMA((dap_size - 1,)),
            pltpu.SemaphoreType.DMA,
            pltpu.SemaphoreType.DMA,
            pltpu.SemaphoreType.DMA,
        ],
        compiler_params=pltpu.CompilerParams(collective_id=0, has_side_effects=True),
    )(*args)
    return result.reshape(tokens, 1, channels)


def fits_small(mesh, shapes):
    pair, lengths, w_bias = shapes[0].shape, shapes[1].shape, shapes[5].shape
    dap_size, slab_size = mesh.shape["dap"], mesh.shape["slab"]
    tokens, width, channels = pair
    rows, cols, heads = tokens // dap_size, width // slab_size, w_bias[1]
    return (
        tokens == width
        and channels == 128
        and rows == 8
        and cols == dap_size == 4
        and tokens == rows * dap_size == cols * slab_size == dap_size * slab_size
        and heads * tokens == channels
        and shapes[7].shape == (channels, channels)
        and tokens % lengths[0] == 0
    )


def solution(mesh):
    in_specs = (P("dap", "slab", None), P(), P(), P(), P(), P(), P(), P())
    out_specs = P(None, ("slab", "dap"), None)

    def run(*args):
        body = on_device_small if fits_small(mesh, args) else on_device
        return jax.shard_map(
            body, mesh=mesh, in_specs=in_specs, out_specs=out_specs, check_vma=False
        )(*args)

    return run
```

```python
import functools
import math

import jax
import jax.numpy as jnp
from jax import lax
from jax.experimental import pallas as pl
from jax.experimental.pallas import tpu as pltpu
from jax.sharding import PartitionSpec as P

MESH = pl.DeviceIdType.MESH
F32 = jnp.float32
BF16 = jnp.bfloat16

EPSILON = 1e-05


def spread_2(value, axis, source):
    kept = jnp.where(lax.axis_index(axis) == source, value, 0).astype(value.dtype)
    return lax.psum(kept, axis)


def layer_norm(values, gain_row):
    average = jnp.mean(values, axis=-1, keepdims=True)
    centred = values - average
    spread = jnp.mean(centred * centred, axis=-1, keepdims=True)
    return centred * lax.rsqrt(spread + EPSILON) * gain_row


def token_valid(chain_lengths, first_token, token_count, slot_size):
    token_index = first_token + jnp.arange(token_count, dtype=jnp.int32)
    chain_index = token_index // slot_size
    member = chain_index[:, None] == jnp.arange(chain_lengths.shape[0], dtype=jnp.int32)[None, :]
    chain_limit = jnp.sum(jnp.where(member, chain_lengths[None, :], 0), axis=1)
    return (token_index % slot_size < chain_limit).astype(jnp.float32)


def on_device(pair, chain_lengths, norm_gains, w_tri_in, w_tri_out, w_bias, w_att_in, w_att_out):
    row_count, col_count, channels = pair.shape
    dap_size = lax.axis_size("dap")
    slab_size = lax.axis_size("slab")
    tokens = row_count * dap_size
    slot_size = tokens // chain_lengths.shape[0]
    dap_index = lax.axis_index("dap")
    slab_index = lax.axis_index("slab")
    row_valid = token_valid(chain_lengths, dap_index * row_count, row_count, slot_size)
    col_valid = token_valid(chain_lengths, slab_index * col_count, col_count, slot_size)
    normed = layer_norm(pair.astype(jnp.float32), norm_gains[0]).astype(jnp.bfloat16)
    projected = jnp.dot(normed, w_tri_in, preferred_element_type=jnp.float32)
    out_gate = jax.nn.sigmoid(projected[..., 4 * channels :])
    normed_all = lax.all_gather(normed, "slab", axis=1, tiled=True)
    slab_ratio = slab_size // dap_size
    offset = slab_index % slab_ratio * col_count
    own_normed = lax.dynamic_slice_in_dim(normed_all, offset, col_count, 0)
    right_normed = spread_2(own_normed, "dap", slab_index // slab_ratio)
    all_valid = token_valid(chain_lengths, 0, tokens, slot_size)
    span = min(128, tokens)
    w_left = w_tri_in[:, : 2 * channels]
    w_right = w_tri_in[:, 2 * channels : 4 * channels]

    def add_span(step, running):
        first = step * span
        k_valid = lax.dynamic_slice_in_dim(all_valid, first, span, 0)
        left_in = lax.dynamic_slice_in_dim(normed_all, first, span, 1)
        right_in = lax.dynamic_slice_in_dim(right_normed, first, span, 1)
        left_proj = jnp.dot(left_in, w_left, preferred_element_type=jnp.float32)
        right_proj = jnp.dot(right_in, w_right, preferred_element_type=jnp.float32)
        left_mask = (row_valid[:, None] * k_valid[None, :])[:, :, None]
        right_mask = (col_valid[:, None] * k_valid[None, :])[:, :, None]
        left_block = (
            left_mask * jax.nn.sigmoid(left_proj[..., channels:]) * left_proj[..., :channels]
        ).astype(jnp.bfloat16)
        right_block = (
            right_mask * jax.nn.sigmoid(right_proj[..., channels:]) * right_proj[..., :channels]
        ).astype(jnp.bfloat16)
        return running + jnp.einsum(
            "ikc,jkc->ijc", left_block, right_block, preferred_element_type=jnp.float32
        )

    triangle = lax.fori_loop(
        0, tokens // span, add_span, jnp.zeros((row_count, col_count, channels), jnp.float32)
    )
    normed_tri = layer_norm(triangle, norm_gains[1]).astype(jnp.bfloat16)
    mixed_update = out_gate * jnp.dot(normed_tri, w_tri_out, preferred_element_type=jnp.float32)
    updated = (pair.astype(jnp.float32) + mixed_update).astype(jnp.bfloat16)
    columns = lax.all_to_all(updated, "dap", split_axis=1, concat_axis=0, tiled=True)
    normed_cols = layer_norm(columns.astype(jnp.float32), norm_gains[2]).astype(jnp.bfloat16)
    normed_rows = layer_norm(updated.astype(jnp.float32), norm_gains[2]).astype(jnp.bfloat16)
    bias_block = jnp.einsum(
        "ijc,ch->hij", normed_rows, w_bias, preferred_element_type=jnp.float32
    ).astype(jnp.bfloat16)
    bias_tall = lax.all_gather(bias_block, "dap", axis=1, tiled=True)
    pair_bias = lax.all_gather(bias_tall, "slab", axis=2, tiled=True)
    att_projected = jnp.dot(normed_cols, w_att_in, preferred_element_type=jnp.float32)
    att_width = w_att_out.shape[0]
    head_count = w_bias.shape[1]
    head_dim = att_width // head_count
    score_scale = 1.0 / math.sqrt(head_dim)
    query_rows = att_projected[..., :att_width].astype(jnp.bfloat16)
    key_rows = att_projected[..., att_width : 2 * att_width].astype(jnp.bfloat16)
    value_rows = att_projected[..., 2 * att_width : 3 * att_width].astype(jnp.bfloat16)
    att_gate = jax.nn.sigmoid(att_projected[..., 3 * att_width :])
    key_valid = token_valid(chain_lengths, 0, tokens, slot_size)[:, None] > 0
    head_outputs = []
    for head_index in range(head_count):
        head_start = head_index * head_dim
        query_head = query_rows[:, 0, head_start : head_start + head_dim]
        key_head = key_rows[:, 0, head_start : head_start + head_dim]
        value_head = value_rows[:, 0, head_start : head_start + head_dim]
        scores = lax.dot_general(
            key_head, query_head, (((1,), (1,)), ((), ())), preferred_element_type=jnp.float32
        ) * score_scale + pair_bias[head_index].astype(jnp.float32)
        scores = jnp.where(key_valid, scores, -1e30)
        score_top = jnp.max(scores, axis=0, keepdims=True)
        weights = jnp.exp(scores - score_top)
        weights = (weights / jnp.sum(weights, axis=0, keepdims=True)).astype(jnp.bfloat16)
        head_outputs.append(
            lax.dot_general(
                weights, value_head, (((0,), (0,)), ((), ())), preferred_element_type=jnp.float32
            )
        )
    column_results = [jnp.concatenate(head_outputs, axis=1)]
    attended = jnp.stack(column_results, axis=1)
    gated = (att_gate * attended).astype(jnp.bfloat16)
    return (
        columns.astype(jnp.float32) + jnp.dot(gated, w_att_out, preferred_element_type=jnp.float32)
    ).astype(jnp.bfloat16)


def small_kernel(
    dap_size, slab_size, slot_size,
    pair_hbm, len_hbm, gains_hbm, w_in_hbm, w_out_hbm, w_bias_hbm, w_att_hbm, w_ao_hbm,
    out_ref,
    pair_v, len_s, gains_v, w_in_v, w_out_v, w_bias_v, w_att_v, w_ao_v,
    x_scr, left_buf, right_own, right_buf, right_f32, upd_own, col_buf, bias_buf,
    in_sem, left_send, left_recv, right_send, right_recv,
    col_send, col_recv, bias_send, bias_recv,
):
    rows, cols, channels = pair_hbm.shape
    block = rows * cols
    tokens = rows * dap_size
    devices = dap_size * slab_size
    ratio = rows // cols
    a = lax.axis_index("dap")
    s = lax.axis_index("slab")
    me = s * dap_size + a

    upper = lax.div(s, slab_size // 2)

    def far_first(n):
        return upper * n + (1 - upper) * (slab_size - 1 - n)

    barrier = pltpu.get_barrier_semaphore()

    def greet(to_a, to_s):
        pl.semaphore_signal(barrier, inc=1, device_id=(to_a, to_s), device_id_type=MESH)

    for n in range(slab_size):
        for d in range(dap_size):
            to_s = far_first(n)
            to_a = lax.rem(a + d, dap_size)
            if d:
                greet(to_a, to_s)
            else:
                pl.when(to_s != s)(functools.partial(greet, to_a, to_s))

    pairs = (
        (pair_hbm, pair_v), (len_hbm, len_s), (gains_hbm, gains_v), (w_in_hbm, w_in_v),
        (w_bias_hbm, w_bias_v), (w_out_hbm, w_out_v), (w_att_hbm, w_att_v), (w_ao_hbm, w_ao_v),
    )
    loads = [pltpu.make_async_copy(src, dst, in_sem.at[n]) for n, (src, dst) in enumerate(pairs)]
    for load in loads:
        load.start()
    for load in loads[:4]:
        load.wait()

    row = lax.broadcasted_iota(jnp.int32, (block, channels), 0)
    lane = lax.broadcasted_iota(jnp.int32, (block, channels), 1)
    row_shift = rows.bit_length() - 1
    col_shift = cols.bit_length() - 1

    def valid(token):
        inside = None
        for chain in range(len_hbm.shape[0]):
            first = chain * slot_size
            here = jnp.logical_and(token >= first, token < first + len_s[chain])
            inside = here if inside is None else jnp.logical_or(inside, here)
        return inside

    def norm(values, gain):
        return layer_norm(values, gains_v[gain : gain + 1, :])

    def norm_parts(values, gain):
        centred = values - jnp.mean(values, axis=-1, keepdims=True)
        spread = jnp.mean(centred * centred, axis=-1, keepdims=True)
        scaled = (centred * gains_v[gain : gain + 1, :]).astype(BF16)
        return scaled, lax.rsqrt(spread + EPSILON)

    def dot(x, y):
        return jnp.dot(x, y, preferred_element_type=F32)

    for i in range(rows):
        x_scr[i * cols : (i + 1) * cols, :] = pair_v[i].astype(F32)
    x_nat = x_scr[...]
    x_perm = jnp.concatenate([x_scr[pl.ds(k, rows, stride=cols), :] for k in range(cols)], axis=0)
    normed_nat = norm(x_nat, 0).astype(BF16)
    normed_perm = norm(x_perm, 0).astype(BF16)
    mask_nat = jnp.logical_and(
        valid(a * rows + lax.shift_right_logical(row, col_shift)),
        valid(s * cols + (row & (cols - 1))),
    ).astype(F32)
    mask_perm = jnp.logical_and(
        valid(a * rows + (row & (rows - 1))),
        valid(s * cols + lax.shift_right_logical(row, row_shift)),
    ).astype(F32)
    left_proj = dot(normed_perm, w_in_v[:, : 2 * channels])
    right_proj = dot(normed_nat, w_in_v[:, 2 * channels : 4 * channels])
    left_buf[s] = (
        mask_perm * jax.nn.sigmoid(left_proj[:, channels:]) * left_proj[:, :channels]
    ).astype(BF16)
    right_own[...] = (
        (mask_nat * jax.nn.sigmoid(right_proj[:, channels:]) * right_proj[:, :channels])
        .astype(BF16)
        .reshape(ratio, block // ratio, channels)
    )

    pl.semaphore_wait(barrier, devices - 1)

    def send_left(to_s):
        pltpu.make_async_remote_copy(
            src_ref=left_buf.at[s],
            dst_ref=left_buf.at[s],
            send_sem=left_send,
            recv_sem=left_recv,
            device_id=(a, to_s),
            device_id_type=MESH,
        ).start()

    def right_copies():
        for part in range(ratio):
            for d in range(dap_size):
                to_a = lax.rem(a + d, dap_size)
                to_s = a * ratio + part
                remote = lambda part=part, d=d, to_a=to_a, to_s=to_s: pltpu.make_async_remote_copy(
                    src_ref=right_own.at[part],
                    dst_ref=right_buf.at[s],
                    send_sem=right_send.at[part * dap_size + d],
                    recv_sem=right_recv,
                    device_id=(to_a, to_s),
                    device_id_type=MESH,
                )
                yield part, to_s, remote, d == 0

    for n in range(slab_size):
        to_left = far_first(n)
        pl.when(to_left != s)(functools.partial(send_left, to_left))
    for part, to_s, remote, maybe_self in right_copies():
        if not maybe_self:
            remote().start()
        else:
            own = pltpu.make_async_copy(right_own.at[part], right_buf.at[s], right_recv)
            pl.when(to_s == s)(own.start)
            pl.when(to_s != s)(lambda: remote().start())

    out_gate = jax.nn.sigmoid(dot(normed_perm, w_in_v[:, 4 * channels :]))
    loads[4].wait()
    heads = w_bias_hbm.shape[0]
    head_dim = channels // heads
    head_shift = head_dim.bit_length() - 1
    spread_row = lax.broadcasted_iota(jnp.int32, (heads, channels), 0)
    spread_lane = lax.broadcasted_iota(jnp.int32, (heads, channels), 1)
    spread = (lax.shift_right_logical(spread_lane, head_shift) == spread_row).astype(F32)
    w_bias_wide = lax.dot_general(
        w_bias_v[...], spread.astype(BF16), (((0,), (0,)), ((), ())), preferred_element_type=F32
    ).astype(BF16)
    key_ok = valid(lane & (tokens - 1))
    lane_head = lax.shift_right_logical(lane, head_shift)
    for load in loads[5:]:
        load.wait()

    pltpu.make_async_copy(right_buf, right_buf, right_recv).wait()
    right_f32[...] = right_buf[...].astype(F32).reshape(right_f32.shape)
    others = left_buf.at[pl.ds(0, slab_size - 1)]
    pltpu.make_async_copy(others, others, left_recv).wait()
    triangle = [jnp.zeros((rows, channels), F32) for _ in range(cols)]
    for k_block in range(slab_size):
        left = left_buf[k_block].astype(F32)
        for k in range(cols):
            left_k = left[k * rows : (k + 1) * rows, :]
            for j in range(cols):
                at = k_block * cols * cols + j * cols + k
                triangle[j] += left_k * right_f32[at : at + 1, :]
    triangle = jnp.concatenate(triangle, axis=0)
    scaled_tri, inverse_tri = norm_parts(triangle, 1)
    mixed_update = out_gate * inverse_tri * dot(scaled_tri, w_out_v[...])
    updated = (x_perm + mixed_update).astype(BF16).astype(F32)
    upd_own[...] = updated.reshape(upd_own.shape)
    col_buf[a] = upd_own[a]

    def col_copy(d):
        to_a = lax.rem(a + d, dap_size)
        return pltpu.make_async_remote_copy(
            src_ref=upd_own.at[to_a],
            dst_ref=col_buf.at[a],
            send_sem=col_send.at[d - 1],
            recv_sem=col_recv,
            device_id=(to_a, s),
            device_id_type=MESH,
        )

    scaled_local, inverse_local = norm_parts(updated, 2)
    bias_all = inverse_local * dot(scaled_local, w_bias_wide)
    bias_row = jnp.sum(
        jnp.where((lane & (block - 1)) == row, bias_all, 0.0), axis=0, keepdims=True
    )
    bias_buf[me] = bias_row.astype(BF16).astype(F32)

    def send_bias(to_a, to_s):
        pltpu.make_async_remote_copy(
            src_ref=bias_buf.at[me],
            dst_ref=bias_buf.at[me],
            send_sem=bias_send,
            recv_sem=bias_recv,
            device_id=(to_a, to_s),
            device_id_type=MESH,
        ).start()

    for n in range(slab_size):
        for d in range(dap_size):
            to_s = far_first(n)
            to_a = lax.rem(a + d, dap_size)
            if d:
                send_bias(to_a, to_s)
            else:
                pl.when(to_s != s)(functools.partial(send_bias, to_a, to_s))

    for d in range(1, dap_size):
        col_copy(d).start()

    other_cols = col_buf.at[pl.ds(0, dap_size - 1)]
    pltpu.make_async_copy(other_cols, other_cols, col_recv).wait()
    columns = col_buf[...].reshape(tokens, channels)
    scaled_cols, inverse_cols = norm_parts(columns, 2)
    projected = inverse_cols * dot(scaled_cols, w_att_v[...])
    query = projected[:, :channels].astype(BF16)
    key = projected[:, channels : 2 * channels].astype(BF16)
    value = projected[:, 2 * channels : 3 * channels].astype(BF16)
    att_gate = jax.nn.sigmoid(projected[:, 3 * channels :])
    blank = jnp.zeros_like(key)
    key_wide = jnp.concatenate([jnp.where(lane_head == h, key, blank) for h in range(heads)], axis=0)
    value_wide = jnp.concatenate(
        [
            jnp.concatenate(
                [
                    jnp.where(lane_head == h, value, blank),
                    (lane_head == h).astype(F32).astype(BF16),
                ],
                axis=1,
            )
            for h in range(heads)
        ],
        axis=0,
    )
    scores = lax.dot_general(
        query, key_wide, (((1,), (1,)), ((), ())), preferred_element_type=F32
    ) * (1.0 / math.sqrt(head_dim))

    other_rows = bias_buf.at[pl.ds(0, devices - 1)]
    pltpu.make_async_copy(other_rows, other_rows, bias_recv).wait()
    got = bias_buf[:, 0, :]
    shift = (row & (cols - 1)) - (lax.shift_right_logical(lane, row_shift) & (dap_size - 1))
    bias = got
    for delta in range(1 - cols, cols):
        if delta:
            moved = pltpu.roll(got, delta % tokens, 0)
            moved = pltpu.roll(moved, (-rows * delta) % channels, 1)
            bias = jnp.where(shift == delta, moved, bias)
    scores = jnp.where(key_ok, scores + bias, -1e30)
    top = jnp.zeros_like(scores)
    for h in range(heads):
        here = lane_head == h
        top = jnp.where(
            here, jnp.max(jnp.where(here, scores, -jnp.inf), axis=1, keepdims=True), top
        )
    weights = jnp.exp(scores - top).astype(BF16)
    summed = dot(weights, value_wide)
    attended = summed[:, :channels] / summed[:, channels:]
    gated = (att_gate * attended).astype(BF16)
    out_ref[...] = (columns + dot(gated, w_ao_v[...])).astype(BF16)

    pltpu.make_async_copy(others, others, left_send).wait()
    for part, to_s, remote, maybe_self in right_copies():
        if not maybe_self:
            remote().wait_send()
        else:
            pl.when(to_s != s)(lambda: remote().wait_send())
    for d in range(1, dap_size):
        col_copy(d).wait_send()
    pltpu.make_async_copy(other_rows, other_rows, bias_send).wait()


def on_device_small(*args):
    pair, chain_lengths = args[:2]
    args = args[:5] + (args[5].T,) + args[6:]
    rows, cols, channels = pair.shape
    dap_size = lax.axis_size("dap")
    slab_size = lax.axis_size("slab")
    tokens = rows * dap_size
    devices = dap_size * slab_size
    block = rows * cols
    ratio = rows // cols
    spaces = [pltpu.VMEM] * 8
    spaces[1] = pltpu.SMEM
    result = pl.pallas_call(
        functools.partial(small_kernel, dap_size, slab_size, tokens // chain_lengths.shape[0]),
        out_shape=pltpu.VMEM((tokens, channels), BF16),
        in_specs=[pl.BlockSpec(memory_space=pl.ANY)] * 8,
        out_specs=pl.BlockSpec(memory_space=pltpu.VMEM),
        scratch_shapes=[space(arg.shape, arg.dtype) for space, arg in zip(spaces, args)]
        + [
            pltpu.VMEM((block, channels), F32),
            pltpu.VMEM((slab_size, block, channels), BF16),
            pltpu.VMEM((ratio, block // ratio, channels), BF16),
            pltpu.VMEM((slab_size, block // ratio, channels), BF16),
            pltpu.VMEM((slab_size * block // ratio, channels), F32),
            pltpu.VMEM((cols, rows, channels), F32),
            pltpu.VMEM((dap_size, rows, channels), F32),
            pltpu.VMEM((devices, 1, channels), F32),
            pltpu.SemaphoreType.DMA((8,)),
            pltpu.SemaphoreType.DMA,
            pltpu.SemaphoreType.DMA,
            pltpu.SemaphoreType.DMA((ratio * dap_size,)),
            pltpu.SemaphoreType.DMA,
            pltpu.SemaphoreType.DMA((dap_size - 1,)),
            pltpu.SemaphoreType.DMA,
            pltpu.SemaphoreType.DMA,
            pltpu.SemaphoreType.DMA,
        ],
        compiler_params=pltpu.CompilerParams(collective_id=0, has_side_effects=True),
    )(*args)
    return result.reshape(tokens, 1, channels)


def fits_small(mesh, shapes):
    pair, lengths, w_bias = shapes[0].shape, shapes[1].shape, shapes[5].shape
    dap_size, slab_size = mesh.shape["dap"], mesh.shape["slab"]
    tokens, width, channels = pair
    rows, cols, heads = tokens // dap_size, width // slab_size, w_bias[1]
    return (
        tokens == width
        and channels == 128
        and rows == 8
        and cols == dap_size == 4
        and tokens == rows * dap_size == cols * slab_size == dap_size * slab_size
        and heads * tokens == channels
        and shapes[7].shape == (channels, channels)
        and tokens % lengths[0] == 0
    )


def solution(mesh):
    in_specs = (P("dap", "slab", None), P(), P(), P(), P(), P(), P(), P())
    out_specs = P(None, ("slab", "dap"), None)

    def run(*args):
        body = on_device_small if fits_small(mesh, args) else on_device
        return jax.shard_map(
            body, mesh=mesh, in_specs=in_specs, out_specs=out_specs, check_vma=False
        )(*args)

    return run
```

```python
import functools
import math

import jax
import jax.numpy as jnp
from jax import lax
from jax.experimental import pallas as pl
from jax.experimental.pallas import tpu as pltpu
from jax.sharding import PartitionSpec as P

MESH = pl.DeviceIdType.MESH
F32 = jnp.float32
BF16 = jnp.bfloat16

EPSILON = 1e-05


def spread_2(value, axis, source):
    kept = jnp.where(lax.axis_index(axis) == source, value, 0).astype(value.dtype)
    return lax.psum(kept, axis)


def layer_norm(values, gain_row):
    average = jnp.mean(values, axis=-1, keepdims=True)
    centred = values - average
    spread = jnp.mean(centred * centred, axis=-1, keepdims=True)
    return centred * lax.rsqrt(spread + EPSILON) * gain_row


def token_valid(chain_lengths, first_token, token_count, slot_size):
    token_index = first_token + jnp.arange(token_count, dtype=jnp.int32)
    chain_index = token_index // slot_size
    member = chain_index[:, None] == jnp.arange(chain_lengths.shape[0], dtype=jnp.int32)[None, :]
    chain_limit = jnp.sum(jnp.where(member, chain_lengths[None, :], 0), axis=1)
    return (token_index % slot_size < chain_limit).astype(jnp.float32)


def on_device(pair, chain_lengths, norm_gains, w_tri_in, w_tri_out, w_bias, w_att_in, w_att_out):
    row_count, col_count, channels = pair.shape
    dap_size = lax.axis_size("dap")
    slab_size = lax.axis_size("slab")
    tokens = row_count * dap_size
    slot_size = tokens // chain_lengths.shape[0]
    dap_index = lax.axis_index("dap")
    slab_index = lax.axis_index("slab")
    row_valid = token_valid(chain_lengths, dap_index * row_count, row_count, slot_size)
    col_valid = token_valid(chain_lengths, slab_index * col_count, col_count, slot_size)
    normed = layer_norm(pair.astype(jnp.float32), norm_gains[0]).astype(jnp.bfloat16)
    projected = jnp.dot(normed, w_tri_in, preferred_element_type=jnp.float32)
    out_gate = jax.nn.sigmoid(projected[..., 4 * channels :])
    normed_all = lax.all_gather(normed, "slab", axis=1, tiled=True)
    slab_ratio = slab_size // dap_size
    offset = slab_index % slab_ratio * col_count
    own_normed = lax.dynamic_slice_in_dim(normed_all, offset, col_count, 0)
    right_normed = spread_2(own_normed, "dap", slab_index // slab_ratio)
    all_valid = token_valid(chain_lengths, 0, tokens, slot_size)
    span = min(128, tokens)
    w_left = w_tri_in[:, : 2 * channels]
    w_right = w_tri_in[:, 2 * channels : 4 * channels]

    def add_span(step, running):
        first = step * span
        k_valid = lax.dynamic_slice_in_dim(all_valid, first, span, 0)
        left_in = lax.dynamic_slice_in_dim(normed_all, first, span, 1)
        right_in = lax.dynamic_slice_in_dim(right_normed, first, span, 1)
        left_proj = jnp.dot(left_in, w_left, preferred_element_type=jnp.float32)
        right_proj = jnp.dot(right_in, w_right, preferred_element_type=jnp.float32)
        left_mask = (row_valid[:, None] * k_valid[None, :])[:, :, None]
        right_mask = (col_valid[:, None] * k_valid[None, :])[:, :, None]
        left_block = (
            left_mask * jax.nn.sigmoid(left_proj[..., channels:]) * left_proj[..., :channels]
        ).astype(jnp.bfloat16)
        right_block = (
            right_mask * jax.nn.sigmoid(right_proj[..., channels:]) * right_proj[..., :channels]
        ).astype(jnp.bfloat16)
        return running + jnp.einsum(
            "ikc,jkc->ijc", left_block, right_block, preferred_element_type=jnp.float32
        )

    triangle = lax.fori_loop(
        0, tokens // span, add_span, jnp.zeros((row_count, col_count, channels), jnp.float32)
    )
    normed_tri = layer_norm(triangle, norm_gains[1]).astype(jnp.bfloat16)
    mixed_update = out_gate * jnp.dot(normed_tri, w_tri_out, preferred_element_type=jnp.float32)
    updated = (pair.astype(jnp.float32) + mixed_update).astype(jnp.bfloat16)
    columns = lax.all_to_all(updated, "dap", split_axis=1, concat_axis=0, tiled=True)
    normed_cols = layer_norm(columns.astype(jnp.float32), norm_gains[2]).astype(jnp.bfloat16)
    normed_rows = layer_norm(updated.astype(jnp.float32), norm_gains[2]).astype(jnp.bfloat16)
    bias_block = jnp.einsum(
        "ijc,ch->hij", normed_rows, w_bias, preferred_element_type=jnp.float32
    ).astype(jnp.bfloat16)
    bias_tall = lax.all_gather(bias_block, "dap", axis=1, tiled=True)
    pair_bias = lax.all_gather(bias_tall, "slab", axis=2, tiled=True)
    att_projected = jnp.dot(normed_cols, w_att_in, preferred_element_type=jnp.float32)
    att_width = w_att_out.shape[0]
    head_count = w_bias.shape[1]
    head_dim = att_width // head_count
    score_scale = 1.0 / math.sqrt(head_dim)
    query_rows = att_projected[..., :att_width].astype(jnp.bfloat16)
    key_rows = att_projected[..., att_width : 2 * att_width].astype(jnp.bfloat16)
    value_rows = att_projected[..., 2 * att_width : 3 * att_width].astype(jnp.bfloat16)
    att_gate = jax.nn.sigmoid(att_projected[..., 3 * att_width :])
    key_valid = token_valid(chain_lengths, 0, tokens, slot_size)[:, None] > 0
    head_outputs = []
    for head_index in range(head_count):
        head_start = head_index * head_dim
        query_head = query_rows[:, 0, head_start : head_start + head_dim]
        key_head = key_rows[:, 0, head_start : head_start + head_dim]
        value_head = value_rows[:, 0, head_start : head_start + head_dim]
        scores = lax.dot_general(
            key_head, query_head, (((1,), (1,)), ((), ())), preferred_element_type=jnp.float32
        ) * score_scale + pair_bias[head_index].astype(jnp.float32)
        scores = jnp.where(key_valid, scores, -1e30)
        score_top = jnp.max(scores, axis=0, keepdims=True)
        weights = jnp.exp(scores - score_top)
        weights = (weights / jnp.sum(weights, axis=0, keepdims=True)).astype(jnp.bfloat16)
        head_outputs.append(
            lax.dot_general(
                weights, value_head, (((0,), (0,)), ((), ())), preferred_element_type=jnp.float32
            )
        )
    column_results = [jnp.concatenate(head_outputs, axis=1)]
    attended = jnp.stack(column_results, axis=1)
    gated = (att_gate * attended).astype(jnp.bfloat16)
    return (
        columns.astype(jnp.float32) + jnp.dot(gated, w_att_out, preferred_element_type=jnp.float32)
    ).astype(jnp.bfloat16)


def small_kernel(
    dap_size, slab_size, slot_size,
    pair_hbm, len_hbm, gains_hbm, w_in_hbm, w_out_hbm, w_bias_hbm, w_att_hbm, w_ao_hbm,
    out_ref,
    pair_v, len_s, gains_v, w_in_v, w_out_v, w_bias_v, w_att_v, w_ao_v,
    x_scr, left_buf, right_own, right_buf, right_f32, upd_own, col_buf, bias_buf,
    in_sem, left_send, left_recv, right_send, right_recv, share_send, share_recv,
    col_send, col_recv, bias_send, bias_recv,
):
    rows, cols, channels = pair_hbm.shape
    block = rows * cols
    tokens = rows * dap_size
    devices = dap_size * slab_size
    ratio = rows // cols
    a = lax.axis_index("dap")
    s = lax.axis_index("slab")
    me = s * dap_size + a

    upper = lax.div(s, slab_size // 2)

    def far_first(n):
        return upper * n + (1 - upper) * (slab_size - 1 - n)

    barrier = pltpu.get_barrier_semaphore()

    def greet(to_a, to_s):
        pl.semaphore_signal(barrier, inc=1, device_id=(to_a, to_s), device_id_type=MESH)

    for n in range(slab_size):
        for d in range(dap_size):
            to_s = far_first(n)
            to_a = lax.rem(a + d, dap_size)
            if d:
                greet(to_a, to_s)
            else:
                pl.when(to_s != s)(functools.partial(greet, to_a, to_s))

    pairs = (
        (pair_hbm, pair_v), (len_hbm, len_s), (gains_hbm, gains_v), (w_in_hbm, w_in_v),
        (w_bias_hbm, w_bias_v), (w_out_hbm, w_out_v), (w_att_hbm, w_att_v), (w_ao_hbm, w_ao_v),
    )
    loads = [pltpu.make_async_copy(src, dst, in_sem.at[n]) for n, (src, dst) in enumerate(pairs)]
    for load in loads:
        load.start()
    for load in loads[:4]:
        load.wait()

    row = lax.broadcasted_iota(jnp.int32, (block, channels), 0)
    lane = lax.broadcasted_iota(jnp.int32, (block, channels), 1)
    row_shift = rows.bit_length() - 1
    col_shift = cols.bit_length() - 1

    def valid(token):
        inside = None
        for chain in range(len_hbm.shape[0]):
            first = chain * slot_size
            here = jnp.logical_and(token >= first, token < first + len_s[chain])
            inside = here if inside is None else jnp.logical_or(inside, here)
        return inside

    def norm(values, gain):
        return layer_norm(values, gains_v[gain : gain + 1, :])

    def norm_parts(values, gain):
        centred = values - jnp.mean(values, axis=-1, keepdims=True)
        spread = jnp.mean(centred * centred, axis=-1, keepdims=True)
        scaled = (centred * gains_v[gain : gain + 1, :]).astype(BF16)
        return scaled, lax.rsqrt(spread + EPSILON)

    def dot(x, y):
        return jnp.dot(x, y, preferred_element_type=F32)

    for i in range(rows):
        x_scr[i * cols : (i + 1) * cols, :] = pair_v[i].astype(F32)
    x_nat = x_scr[...]
    x_perm = jnp.concatenate([x_scr[pl.ds(k, rows, stride=cols), :] for k in range(cols)], axis=0)
    normed_nat = norm(x_nat, 0).astype(BF16)
    normed_perm = norm(x_perm, 0).astype(BF16)
    mask_nat = jnp.logical_and(
        valid(a * rows + lax.shift_right_logical(row, col_shift)),
        valid(s * cols + (row & (cols - 1))),
    ).astype(F32)
    mask_perm = jnp.logical_and(
        valid(a * rows + (row & (rows - 1))),
        valid(s * cols + lax.shift_right_logical(row, row_shift)),
    ).astype(F32)
    left_proj = dot(normed_perm, w_in_v[:, : 2 * channels])
    right_proj = dot(normed_nat, w_in_v[:, 2 * channels : 4 * channels])
    left_buf[s] = (
        mask_perm * jax.nn.sigmoid(left_proj[:, channels:]) * left_proj[:, :channels]
    ).astype(BF16)
    right_own[...] = (
        (mask_nat * jax.nn.sigmoid(right_proj[:, channels:]) * right_proj[:, :channels])
        .astype(BF16)
        .reshape(ratio, block // ratio, channels)
    )

    pl.semaphore_wait(barrier, devices - 1)

    def send_left(to_s):
        pltpu.make_async_remote_copy(
            src_ref=left_buf.at[s],
            dst_ref=left_buf.at[s],
            send_sem=left_send,
            recv_sem=left_recv,
            device_id=(a, to_s),
            device_id_type=MESH,
        ).start()

    slot = lax.rem(s, 2) * (slab_size // 2) + lax.div(s, 2)

    def right_copies():
        for part in range(ratio):
            for d in range(dap_size // 2):
                to_a = lax.rem(lax.div(a, 2) + d, dap_size // 2) * 2 + lax.rem(s, 2)
                to_s = a * ratio + part
                same = jnp.logical_and(to_s == s, to_a == a)
                remote = lambda part=part, d=d, to_a=to_a, to_s=to_s: pltpu.make_async_remote_copy(
                    src_ref=right_own.at[part],
                    dst_ref=right_buf.at[slot],
                    send_sem=right_send.at[part * (dap_size // 2) + d],
                    recv_sem=right_recv,
                    device_id=(to_a, to_s),
                    device_id_type=MESH,
                )
                yield part, same, remote, d == 0

    for part, same, remote, maybe_self in right_copies():
        if not maybe_self:
            remote().start()
        else:
            own = pltpu.make_async_copy(right_own.at[part], right_buf.at[slot], right_recv)
            pl.when(same)(own.start)
            pl.when(jnp.logical_not(same))(lambda: remote().start())

    for n in range(slab_size):
        to_left = far_first(n)
        pl.when(to_left != s)(functools.partial(send_left, to_left))

    out_gate = jax.nn.sigmoid(dot(normed_perm, w_in_v[:, 4 * channels :]))
    loads[4].wait()
    heads = w_bias_hbm.shape[0]
    head_dim = channels // heads
    head_shift = head_dim.bit_length() - 1
    spread_row = lax.broadcasted_iota(jnp.int32, (heads, channels), 0)
    spread_lane = lax.broadcasted_iota(jnp.int32, (heads, channels), 1)
    spread = (lax.shift_right_logical(spread_lane, head_shift) == spread_row).astype(F32)
    w_bias_wide = lax.dot_general(
        w_bias_v[...], spread.astype(BF16), (((0,), (0,)), ((), ())), preferred_element_type=F32
    ).astype(BF16)
    key_ok = valid(lane & (tokens - 1))
    lane_head = lax.shift_right_logical(lane, head_shift)
    for load in loads[5:]:
        load.wait()

    half = right_buf.at[pl.ds(0, slab_size // 2)]
    core = lax.rem(a, 2)
    mine = right_buf.at[pl.ds(core * (slab_size // 2), slab_size // 2)]
    pltpu.make_async_copy(half, half, right_recv).wait()
    share = pltpu.make_async_remote_copy(
        src_ref=mine,
        dst_ref=mine,
        send_sem=share_send,
        recv_sem=share_recv,
        device_id=(a + 1 - 2 * core, s),
        device_id_type=MESH,
    )
    share.start()
    share.wait_recv()
    right_f32[...] = right_buf[...].astype(F32).reshape(right_f32.shape)
    others = left_buf.at[pl.ds(0, slab_size - 1)]
    pltpu.make_async_copy(others, others, left_recv).wait()
    triangle = [jnp.zeros((rows, channels), F32) for _ in range(cols)]
    for k_block in range(slab_size):
        left = left_buf[k_block].astype(F32)
        for k in range(cols):
            left_k = left[k * rows : (k + 1) * rows, :]
            for j in range(cols):
                k_slot = k_block % 2 * (slab_size // 2) + k_block // 2
                at = k_slot * cols * cols + j * cols + k
                triangle[j] += left_k * right_f32[at : at + 1, :]
    triangle = jnp.concatenate(triangle, axis=0)
    scaled_tri, inverse_tri = norm_parts(triangle, 1)
    mixed_update = out_gate * inverse_tri * dot(scaled_tri, w_out_v[...])
    updated = (x_perm + mixed_update).astype(BF16).astype(F32)
    upd_own[...] = updated.reshape(upd_own.shape)
    col_buf[a] = upd_own[a]

    def col_copy(d):
        to_a = lax.rem(a + d, dap_size)
        return pltpu.make_async_remote_copy(
            src_ref=upd_own.at[to_a],
            dst_ref=col_buf.at[a],
            send_sem=col_send.at[d - 1],
            recv_sem=col_recv,
            device_id=(to_a, s),
            device_id_type=MESH,
        )

    scaled_local, inverse_local = norm_parts(updated, 2)
    bias_all = inverse_local * dot(scaled_local, w_bias_wide)
    bias_row = jnp.sum(
        jnp.where((lane & (block - 1)) == row, bias_all, 0.0), axis=0, keepdims=True
    )
    bias_buf[me] = bias_row.astype(BF16).astype(F32)

    def send_bias(to_a, to_s):
        pltpu.make_async_remote_copy(
            src_ref=bias_buf.at[me],
            dst_ref=bias_buf.at[me],
            send_sem=bias_send,
            recv_sem=bias_recv,
            device_id=(to_a, to_s),
            device_id_type=MESH,
        ).start()

    for n in range(slab_size):
        for d in range(dap_size):
            to_s = far_first(n)
            to_a = lax.rem(a + d, dap_size)
            if d:
                send_bias(to_a, to_s)
            else:
                pl.when(to_s != s)(functools.partial(send_bias, to_a, to_s))

    for d in range(1, dap_size):
        col_copy(d).start()

    other_cols = col_buf.at[pl.ds(0, dap_size - 1)]
    pltpu.make_async_copy(other_cols, other_cols, col_recv).wait()
    columns = col_buf[...].reshape(tokens, channels)
    scaled_cols, inverse_cols = norm_parts(columns, 2)
    projected = inverse_cols * dot(scaled_cols, w_att_v[...])
    query = projected[:, :channels].astype(BF16)
    key = projected[:, channels : 2 * channels].astype(BF16)
    value = projected[:, 2 * channels : 3 * channels].astype(BF16)
    att_gate = jax.nn.sigmoid(projected[:, 3 * channels :])
    blank = jnp.zeros_like(key)
    key_wide = jnp.concatenate([jnp.where(lane_head == h, key, blank) for h in range(heads)], axis=0)
    value_wide = jnp.concatenate(
        [
            jnp.concatenate(
                [
                    jnp.where(lane_head == h, value, blank),
                    (lane_head == h).astype(F32).astype(BF16),
                ],
                axis=1,
            )
            for h in range(heads)
        ],
        axis=0,
    )
    scores = lax.dot_general(
        query, key_wide, (((1,), (1,)), ((), ())), preferred_element_type=F32
    ) * (1.0 / math.sqrt(head_dim))

    other_rows = bias_buf.at[pl.ds(0, devices - 1)]
    pltpu.make_async_copy(other_rows, other_rows, bias_recv).wait()
    got = bias_buf[:, 0, :]
    shift = (row & (cols - 1)) - (lax.shift_right_logical(lane, row_shift) & (dap_size - 1))
    bias = got
    for delta in range(1 - cols, cols):
        if delta:
            moved = pltpu.roll(got, delta % tokens, 0)
            moved = pltpu.roll(moved, (-rows * delta) % channels, 1)
            bias = jnp.where(shift == delta, moved, bias)
    scores = jnp.where(key_ok, scores + bias, -1e30)
    top = jnp.zeros_like(scores)
    for h in range(heads):
        here = lane_head == h
        top = jnp.where(
            here, jnp.max(jnp.where(here, scores, -jnp.inf), axis=1, keepdims=True), top
        )
    weights = jnp.exp(scores - top).astype(BF16)
    summed = dot(weights, value_wide)
    attended = summed[:, :channels] / summed[:, channels:]
    gated = (att_gate * attended).astype(BF16)
    out_ref[...] = (columns + dot(gated, w_ao_v[...])).astype(BF16)

    share.wait_send()
    pltpu.make_async_copy(others, others, left_send).wait()
    for part, same, remote, maybe_self in right_copies():
        if not maybe_self:
            remote().wait_send()
        else:
            pl.when(jnp.logical_not(same))(lambda: remote().wait_send())
    for d in range(1, dap_size):
        col_copy(d).wait_send()
    pltpu.make_async_copy(other_rows, other_rows, bias_send).wait()


def on_device_small(*args):
    pair, chain_lengths = args[:2]
    args = args[:5] + (args[5].T,) + args[6:]
    rows, cols, channels = pair.shape
    dap_size = lax.axis_size("dap")
    slab_size = lax.axis_size("slab")
    tokens = rows * dap_size
    devices = dap_size * slab_size
    block = rows * cols
    ratio = rows // cols
    spaces = [pltpu.VMEM] * 8
    spaces[1] = pltpu.SMEM
    result = pl.pallas_call(
        functools.partial(small_kernel, dap_size, slab_size, tokens // chain_lengths.shape[0]),
        out_shape=pltpu.VMEM((tokens, channels), BF16),
        in_specs=[pl.BlockSpec(memory_space=pl.ANY)] * 8,
        out_specs=pl.BlockSpec(memory_space=pltpu.VMEM),
        scratch_shapes=[space(arg.shape, arg.dtype) for space, arg in zip(spaces, args)]
        + [
            pltpu.VMEM((block, channels), F32),
            pltpu.VMEM((slab_size, block, channels), BF16),
            pltpu.VMEM((ratio, block // ratio, channels), BF16),
            pltpu.VMEM((slab_size, block // ratio, channels), BF16),
            pltpu.VMEM((slab_size * block // ratio, channels), F32),
            pltpu.VMEM((cols, rows, channels), F32),
            pltpu.VMEM((dap_size, rows, channels), F32),
            pltpu.VMEM((devices, 1, channels), F32),
            pltpu.SemaphoreType.DMA((8,)),
            pltpu.SemaphoreType.DMA,
            pltpu.SemaphoreType.DMA,
            pltpu.SemaphoreType.DMA((ratio * (dap_size // 2),)),
            pltpu.SemaphoreType.DMA,
            pltpu.SemaphoreType.DMA,
            pltpu.SemaphoreType.DMA,
            pltpu.SemaphoreType.DMA((dap_size - 1,)),
            pltpu.SemaphoreType.DMA,
            pltpu.SemaphoreType.DMA,
            pltpu.SemaphoreType.DMA,
        ],
        compiler_params=pltpu.CompilerParams(collective_id=0, has_side_effects=True),
    )(*args)
    return result.reshape(tokens, 1, channels)


def fits_small(mesh, shapes):
    pair, lengths, w_bias = shapes[0].shape, shapes[1].shape, shapes[5].shape
    dap_size, slab_size = mesh.shape["dap"], mesh.shape["slab"]
    tokens, width, channels = pair
    rows, cols, heads = tokens // dap_size, width // slab_size, w_bias[1]
    return (
        tokens == width
        and channels == 128
        and rows == 8
        and cols == dap_size == 4
        and tokens == rows * dap_size == cols * slab_size == dap_size * slab_size
        and heads * tokens == channels
        and shapes[7].shape == (channels, channels)
        and tokens % lengths[0] == 0
    )


def solution(mesh):
    in_specs = (P("dap", "slab", None), P(), P(), P(), P(), P(), P(), P())
    out_specs = P(None, ("slab", "dap"), None)

    def run(*args):
        body = on_device_small if fits_small(mesh, args) else on_device
        return jax.shard_map(
            body, mesh=mesh, in_specs=in_specs, out_specs=out_specs, check_vma=False
        )(*args)

    return run
```
